32 devices in a mesh: dp: 8 (over z, x), tensor: 4 (over y, core).
Axes of the slice: x: 2, y: 2, z: 4, core: 2. Of those that a mesh axis runs over, the one named last changes fastest.
Arguments:
- layer_input: bfloat16 [16, 1024, 768], P('dp', 'tensor'), may hold values from -6 to 6
- cotangent: bfloat16 [16, 1024, 768], P('dp', 'tensor'), may hold values from -6 to 6
- segment_ids: int32 [16, 1024], P('dp'), may hold values from 0 to 3, never falling along the last dimension, each value on 1 to 512 neighbouring positions
- norm_gains: float32 [2, 768], replicated, may hold values from 0.5 to 1.5
- norm_biases: float32 [2, 768], replicated, may hold values from -2 to 2
- attend_weight: bfloat16 [3, 768, 768], P(None, None, 'tensor'), may hold values from -0.21875 to 0.21875
- output_weight: bfloat16 [768, 768], P('tensor'), may hold values from -1.75 to 1.75
- expand_weight: bfloat16 [768, 3072], P(None, 'tensor'), may hold values from -0.21875 to 0.21875
- shrink_weight: bfloat16 [3072, 768], P('tensor'), may hold values from -0.109375 to 0.109375
Outputs:
- layer_output: bfloat16 [16, 1024, 768], P('dp', 'tensor')
- input_grad: bfloat16 [16, 1024, 768], P('dp', 'tensor')
- grad_gains: float32 [2, 768], replicated
- grad_biases: float32 [2, 768], replicated
- grad_attend: float32 [3, 768, 768], P(None, None, 'tensor')
- grad_output: float32 [768, 768], P('tensor')
- grad_expand: float32 [768, 3072], P(None, 'tensor')
- grad_shrink: float32 [3072, 768], P('tensor')
- kept_fraction: float32 [], replicated
The draws below stay inside these ranges and needn't reach their ends.
Inputs may be any that keep to these rules, and one draw needn't show every extreme that they name: `segment_ids`: in each row the document numbers never fall and every one of the 4 numbers appears; each document holds at most 512 tokens, and one of every row holds exactly that many.
All inputs are finite; a program needn't handle non-finite values.
Results may differ from the reference program's by a relative error of at most 0.012.
The reference program's roundings to bfloat16 on the way count: a program that leaves them out, or rounds other values in their place, can miss the bound.
Values may be sent and summed in bfloat16 or wider, within the bound.
No kernel may reach another device: no remote copies, remote signals or barrier semaphores. Data moves between devices by JAX's collectives and lax.ppermute only.
A program may use at most 192 MiB of HBM per device.

```python
import math
import jax
import jax.numpy as jnp
import numpy as np
from jax import lax

D = 768
HEAD_COUNT = 12
HEAD_DIM = 64
FF = 3072
SEQ = 1024
DOCS = 4
ROWS = 16
N_TENSOR = 4


def steps_of(own_key, extent, shards, low, top_value):
    factor_of, own = 1.0, jax.random.fold_in(own_key, 6)
    for dim, shards_of in shards:
        steps = jnp.exp(jax.random.uniform(jax.random.fold_in(own, dim), (shards_of,), jnp.float32, low / len(shards), top_value / len(shards)))
        factor_of = factor_of * jnp.repeat(steps, extent[dim] // shards_of).reshape([-1 if axis == dim else 1 for axis in range(len(extent))])
    return factor_of


def length_profile(count, total, limit, lean):
    portions = [(1 << 20) // math.isqrt(standing ** lean) + 1 for standing in range(2, count + 1)]
    spare, given = total - limit - (count - 1), [1] * (count - 1)
    while spare > 0:
        candidates = [i for i in range(count - 1) if given[i] < limit]
        whole, left = sum([portions[i] for i in candidates]), spare
        for i in candidates:
            extra = min(limit - given[i], max(1, left * portions[i] // whole), spare)
            given[i] = given[i] + extra
            spare = spare - extra
    return np.array([limit] + given)


def uneven(rng, count, total, most, skew):
    if count == 2:
        one = jax.random.randint(rng, (), max(1, total - most), min(most, total - 1) + 1)
        return jnp.stack([one, total - one])
    sizes = jnp.asarray(length_profile(count, total, most, skew), jnp.int32)
    pairs = (count - 1) // 2
    donor, sink = sizes[1:1 + 2 * pairs:2], sizes[2:2 + 2 * pairs:2]
    room = jnp.minimum(donor - 1, most - sink)
    passed = jax.random.randint(jax.random.fold_in(rng, 1), (pairs,), 0, 1 << 20) % (room + 1)
    sizes = sizes.at[1:1 + 2 * pairs:2].set(donor - passed).at[2:2 + 2 * pairs:2].set(sink + passed)
    return sizes[jax.random.permutation(jax.random.fold_in(rng, 2), count)]


def bell_draw(key, dims, spread, reach, split=(), dtype=jnp.bfloat16):
    loudness = steps_of(key, dims, split, -0.22, 0.18) if split else 1.0
    array = jax.random.normal(key, dims, jnp.float32) * spread * loudness
    return jnp.minimum(jnp.maximum(array, -reach), reach).astype(dtype)


def setup_inputs(seed: int = 0) -> dict:
    keys = jax.random.split(jax.random.key(seed), 10)
    return {
        "layer_input": bell_draw(keys[0], (ROWS, SEQ, D), 1.0, 6.0, ((0, 8), (1, 4))),
        "cotangent": bell_draw(keys[1], (ROWS, SEQ, D), 1.0, 6.0, ((0, 8), (1, 4))),
        "segment_ids": jax.vmap(lambda own: jnp.searchsorted(jnp.cumsum(uneven(own, DOCS, SEQ, SEQ // 2, 0)), jnp.arange(SEQ), side="right"))(jax.random.split(keys[2], ROWS)).reshape((ROWS, SEQ)).astype(jnp.int32),
        "norm_gains": jnp.clip(1.0 + 0.1 * jax.random.normal(keys[3], (2, D), jnp.float32), 0.5, 1.5),
        "norm_biases": bell_draw(keys[4], (2, D), 0.3, 2.0, (), jnp.float32),
        "attend_weight": bell_draw(keys[5], (3, D, D), D ** -0.5, 0.21875, ((2, 4),)),
        "output_weight": bell_draw(keys[6], (D, D), (D // 64) ** -0.5, 1.75, ((0, 4),)),
        "expand_weight": bell_draw(keys[7], (D, FF), D ** -0.5, 0.21875, ((1, 4),)),
        "shrink_weight": bell_draw(keys[8], (FF, D), FF ** -0.5, 0.109375, ((0, 4),)),
    }


EPSILON = 1e-05
SELECT_SCALE = 0.02
THRESHOLD = 4.0
MASKED_FILL = -1e+30
PRECISE = lax.Precision.HIGHEST

@jax.custom_vjp
def low(v):
    return lax.optimization_barrier(v.astype(jnp.bfloat16)).astype(jnp.float32)

@jax.custom_vjp
def low_back(v):
    return v

def low_keep(v):
    return (low(v), None)

def low_pass(kept, grad):
    return (grad,)

def back_keep(v):
    return (v, None)

def back_low(kept, grad):
    return (low(grad),)
low.defvjp(low_keep, low_pass)
low_back.defvjp(back_keep, back_low)

def layer_norm(values, gains, shifts):
    average = lax.optimization_barrier(jnp.mean(values, axis=-1, keepdims=True))
    centred = values - average
    variance = lax.optimization_barrier(jnp.mean(centred * centred, axis=-1, keepdims=True))
    return centred * lax.rsqrt(variance + EPSILON) * gains + shifts

def forward_row(row_input, document_segments, gains, biases, attend, output, expand, shrink):
    places = jnp.arange(SEQ)
    same_doc = document_segments[:, None] == document_segments[None, :]
    visible = same_doc & (places[None, :] <= places[:, None])
    strict = (same_doc & (places[None, :] < places[:, None])).astype(jnp.float32)
    factor = HEAD_DIM ** (-0.5)
    first_normed_rows = low(layer_norm(row_input, gains[0], biases[0]))
    projected = low_back(low(jnp.einsum('sd,cde->cse', first_normed_rows, attend, precision=PRECISE)))
    heads = projected.reshape(3, SEQ, HEAD_COUNT, HEAD_DIM)
    queries = heads[0]
    key_heads = heads[1]
    values = heads[2]
    scores = low_back(jnp.einsum('qhe,khe->hqk', queries, key_heads, precision=PRECISE) * factor)
    penalty_rows = []
    chosen_list = []
    for member in range(N_TENSOR):
        select = low_back(jnp.einsum('qe,ke->qk', queries[:, 0], key_heads[:, 0], precision=PRECISE) * factor)
        chosen_index = SELECT_SCALE * jax.nn.softplus(select) * strict
        chosen_list.append(chosen_index)
        penalty_rows.append(jnp.cumsum(chosen_index, axis=0) - chosen_index)
    fraction_part = jnp.sum(jax.nn.sigmoid(lax.optimization_barrier(jnp.sum(chosen_list[0], axis=0)) - THRESHOLD))
    selection_penalty = jnp.repeat(jnp.stack(penalty_rows), HEAD_COUNT // N_TENSOR, axis=0)
    logits = jnp.where(visible[None], scores - selection_penalty, MASKED_FILL)
    chances = low(jax.nn.softmax(logits, axis=-1))
    attended = jnp.einsum('hqk,khe->qhe', chances, values, precision=PRECISE).reshape(SEQ, D)
    attended = low_back(low(attended))
    middle = row_input + low_back(jnp.dot(attended, output, precision=PRECISE))
    normed_second = low(layer_norm(middle, gains[1], biases[1]))
    hidden = low_back(jnp.dot(normed_second, expand, precision=PRECISE))
    active = low(jax.nn.gelu(hidden, approximate=True))
    return (middle + jnp.dot(active, shrink, precision=PRECISE), fraction_part)

def reference(layer_input, cotangent, segment_ids, norm_gains, norm_biases, attend_weight, output_weight, expand_weight, shrink_weight):
    params = tuple((jnp.asarray(argument).astype(jnp.float32) for argument in (norm_gains, norm_biases, attend_weight, output_weight, expand_weight, shrink_weight)))

    def one_row(running, row_data):
        row_input, row_cotangent, row_segments = row_data

        def forward(row_values, gains, biases, attend, output, expand, shrink):
            return forward_row(row_values, row_segments, gains, biases, attend, output, expand, shrink)
        result, pullback, fraction_part = jax.vjp(forward, row_input.astype(jnp.float32), *params, has_aux=True)
        gradients = pullback(row_cotangent.astype(jnp.float32))
        updated = tuple((running[index] + gradients[index + 1] for index in range(6))) + (running[6] + fraction_part,)
        return (updated, (result.astype(jnp.bfloat16), gradients[0].astype(jnp.bfloat16)))
    initial = tuple((jnp.zeros_like(weight_item) for weight_item in params)) + (jnp.zeros((), jnp.float32),)
    running, (outputs, input_grads) = lax.scan(one_row, initial, (layer_input, cotangent, segment_ids))
    kept_fraction = running[6] / (ROWS * SEQ)
    return (outputs, input_grads, running[0], running[1], running[2], running[3], running[4], running[5], kept_fraction)
```

```python
from functools import partial

import jax
import jax.numpy as jnp
from jax import lax
from jax.experimental import pallas as pl
from jax.experimental.pallas import tpu as pltpu
from jax.sharding import PartitionSpec as P

HEAD_DIM = 64
EPSILON = 1e-05
SELECT_SCALE = 0.02
THRESHOLD = 4.0
GELU_A = 0.7978845608028654
GELU_B = 0.044715
BF = jnp.bfloat16
F32 = jnp.float32


def mm(spec, a, b):
    return jnp.einsum(spec, a, b, preferred_element_type=F32)


def standardize(values):
    average = jnp.mean(values, axis=-1, keepdims=True)
    centred = values - average
    variance = jnp.mean(centred * centred, axis=-1, keepdims=True)
    scale = lax.rsqrt(variance + EPSILON)
    return centred * scale, scale


def norm_back(grad, standard, scale, gains):
    inner = grad * gains
    return scale * (
        inner
        - jnp.mean(inner, axis=-1, keepdims=True)
        - standard * jnp.mean(inner * standard, axis=-1, keepdims=True)
    )


TILE = 256
WIDE = 512
HALF = 128
CHUNK = 32
REACH = 2
BIG = 1e30


def dot(a, b, dims=((1,), (0,))):
    return lax.dot_general(a, b, (dims, ((), ())), preferred_element_type=F32)


def dot_t(a, b):
    return dot(a, b, ((1,), (1,)))


def window(tile):
    start = max(0, tile - REACH) * TILE
    return start, (tile + 1) * TILE - start


def half_columns(tile, half):
    start, span = window(tile)
    first = max(0, tile * TILE + half * HALF - REACH * TILE) - start
    return first, span - HALF if half == 0 else span


def chunks(tile, size=CHUNK):
    for half in range(2):
        first, last = half_columns(tile, half)
        for row in range(half * HALF, (half + 1) * HALF, size):
            yield row, first, last


def clear_unseen(tile, ref):
    start, span = window(tile)
    for half in range(2):
        first, last = half_columns(tile, half)
        rows = slice(half * HALF, (half + 1) * HALF)
        if first > 0:
            ref[rows, :first] = jnp.zeros((HALF, first), ref.dtype)
        if last < span:
            ref[rows, last:span] = jnp.zeros((HALF, span - last), ref.dtype)


def flip(v):
    return ((v & 1) << 1) | (v >> 1)


def slot_rows(block, t):
    return pl.ds(pl.multiple_of(flip(block ^ t) * TILE, TILE), TILE)


def block_rows(slot, t):
    return pl.ds(pl.multiple_of((flip(slot) ^ t) * TILE, TILE), TILE)


def lane_mask(shape, head):
    lanes = lax.broadcasted_iota(jnp.int32, shape, 1)
    return lanes < HEAD_DIM if head == 0 else lanes >= HEAD_DIM


def of_head(value, head):
    if head == 2:
        return value[:, 2 * HEAD_DIM :]
    pair = value[:, : 2 * HEAD_DIM]
    return jnp.where(lane_mask(pair.shape, head), pair, jnp.zeros_like(pair))


def with_head(value, head):
    return value[:, 2 * HEAD_DIM :] if head == 2 else value[:, : 2 * HEAD_DIM]


def join_heads(parts):
    pair = jnp.where(lane_mask(parts[0].shape, 0), parts[0], parts[1])
    return pair, parts[2]


def triangle(upper):
    rows = lax.broadcasted_iota(jnp.int32, (TILE, TILE), 0)
    columns = lax.broadcasted_iota(jnp.int32, (TILE, TILE), 1)
    inside = columns > rows if upper else columns < rows
    return inside.astype(F32).astype(BF)


def split_store(value, high_ref, low_ref, rows, columns):
    high = value.astype(BF)
    high_ref[rows, columns] = high
    low_ref[rows, columns] = (value - high.astype(F32)).astype(BF)


def place(t, result, out_ref, c):
    if c == 0:
        result = result.astype(BF).astype(F32) * (HEAD_DIM ** -0.5)
    result = result.astype(BF)
    for slot in range(result.shape[0] // TILE):
        out_ref[c, block_rows(slot, t), :] = result[slot * TILE : (slot + 1) * TILE]


def project(t, rows_ref, weight_ref, out_ref):
    for c in range(3):
        place(t, dot_t(rows_ref[...], weight_ref[c]), out_ref, c)


def attend_group(t, qkv_ref, pm_ref, att_ref, lse_ref, s_ref, p_ref, size):
    length = qkv_ref.shape[1]
    for tile in range(length // TILE):
        start, span = window(tile)
        here = slice(tile * TILE, (tile + 1) * TILE)
        keys = qkv_ref[1, start : start + span]
        values = qkv_ref[2, start : start + span]
        queries = qkv_ref[0, here]
        outs = []
        for head in range(3):
            s_ref[head, :, :span] = dot_t(of_head(queries, head), with_head(keys, head))
            clear_unseen(tile, p_ref.at[head])
            for row, first, last in chunks(tile, size):
                rows = slice(row, row + size)
                logits = (
                    s_ref[head, rows, first:last]
                    - pm_ref[tile * TILE + row : tile * TILE + row + size, first:last]
                )
                highest = jnp.max(logits, axis=1, keepdims=True)
                powers = jnp.exp(logits - highest)
                total = jnp.sum(powers, axis=1, keepdims=True)
                p_ref[head, rows, first:last] = (powers * (1.0 / total)).astype(BF)
                lse_ref[tile * TILE + row : tile * TILE + row + size, head : head + 1] = (
                    highest + jnp.log(total)
                )
            outs.append(dot(p_ref[head, :, :span], with_head(values, head)))
        pair, last_head = join_heads(outs)
        where = slot_rows(tile, t)
        att_ref[where, : 2 * HEAD_DIM] = pair.astype(BF)
        att_ref[where, 2 * HEAD_DIM :] = last_head.astype(BF)


def first_kernel(
    t_ref, x_own_ref, x_oth_ref, gains_ref, biases_ref, weight_ref, seg_ref,
    rows_ref, qkv_ref, zqk_ref, pm_ref, att_ref, lse_ref, kept_ref, zero_ref,
    s_ref, p_ref, high_ref, low_ref, carry_ref, seg_col_ref,
):
    t = t_ref[0]
    length = rows_ref.shape[0]
    half = length // 2
    for part, ref in enumerate((x_own_ref, x_oth_ref)):
        for row in range(0, half, HALF):
            standard, _ = standardize(ref[row : row + HALF].astype(F32))
            rows_ref[part * half + row : part * half + row + HALF] = (
                standard * gains_ref[0:1] + biases_ref[0:1]
            ).astype(BF)
    zero_ref[...] = jnp.where(t % 2 == 0, x_own_ref[half:], x_oth_ref[half:])
    for c in range(2):
        weight = zero_ref[c * HEAD_DIM : (c + 1) * HEAD_DIM]
        place(t, dot_t(rows_ref[...], weight), zqk_ref, c)
    project(t, rows_ref, weight_ref, qkv_ref)
    for ref in (rows_ref, zqk_ref, qkv_ref, zero_ref):
        complete(ref)
    for tile in range(length // TILE):
        here = slice(tile * TILE, (tile + 1) * TILE)
        seg_col_ref[here] = jnp.broadcast_to(seg_ref[:, here], (8, TILE)).T
    lower = triangle(False)
    carry_ref[...] = jnp.zeros_like(carry_ref)
    for tile in range(length // TILE):
        start, span = window(tile)
        s_ref[0, :, :span] = dot_t(
            zqk_ref[0, tile * TILE : (tile + 1) * TILE], zqk_ref[1, start : start + span]
        )
        clear_unseen(tile, high_ref)
        clear_unseen(tile, low_ref)
        last_row = None
        for row, first, last in chunks(tile):
            rows = slice(row, row + CHUNK)
            select = s_ref[0, rows, first:last]
            soft = jnp.maximum(select, 0.0) + jnp.log1p(jnp.exp(-jnp.abs(select)))
            at = tile * TILE + row
            query = at + lax.broadcasted_iota(jnp.int32, select.shape, 0)
            key = start + first + lax.broadcasted_iota(jnp.int32, select.shape, 1)
            same = seg_col_ref[at : at + CHUNK, :1] == seg_ref[:, start + first : start + last]
            chosen = jnp.where(same & (key < query), SELECT_SCALE * soft, 0.0)
            split_store(chosen, high_ref, low_ref, rows, slice(first, last))
            last_row = chosen[CHUNK - 1 :]
        carry = carry_ref[:, start : start + span]
        inner = dot(lower, high_ref[:, :span]) + dot(lower, low_ref[:, :span])
        s_ref[1, :, :span] = inner + carry
        carry_ref[:, start : start + span] = carry + inner[TILE - 1 :]
        carry_ref[:, start + first : start + last] += last_row
        for row, first, last in chunks(tile):
            rows = slice(row, row + CHUNK)
            at = tile * TILE + row
            shape = (CHUNK, last - first)
            query = at + lax.broadcasted_iota(jnp.int32, shape, 0)
            key = start + first + lax.broadcasted_iota(jnp.int32, shape, 1)
            same = seg_col_ref[at : at + CHUNK, :1] == seg_ref[:, start + first : start + last]
            pm_ref[at : at + CHUNK, first:last] = jnp.where(
                same & (key <= query), s_ref[1, rows, first:last], BIG
            )
    kept = jnp.sum(jax.nn.sigmoid(carry_ref[...] - THRESHOLD), axis=1, keepdims=True)
    kept_ref[...] = jnp.broadcast_to(kept, kept_ref.shape)
    complete(pm_ref)
    attend_group(t, qkv_ref, pm_ref, att_ref, lse_ref, s_ref, p_ref, 16)


def second_kernel(
    t_ref, rows_ref, own_ref, far_ref, pm_ref, att_own_ref,
    qkv_ref, att_ref, lse_ref, branch_ref, send_ref,
    s_ref, p_ref,
):
    t = t_ref[0]
    project(t, rows_ref, far_ref, qkv_ref)
    complete(qkv_ref)
    attend_group(t, qkv_ref, pm_ref, att_ref, lse_ref, s_ref, p_ref, 64)
    complete(att_ref)
    complete(lse_ref)
    for row in range(0, rows_ref.shape[0], TILE):
        here = slice(row, row + TILE)
        branch = dot(att_own_ref[here], own_ref[...]) + dot(
            att_ref[here], far_ref[3]
        )
        branch_ref[here] = branch
        send_ref[here] = branch.astype(BF)


def backward_kernel(
    chained, t_ref, qkv_ref, zqk_ref, pm_ref, lse_ref, grad_ref, *refs
):
    before_ref, refs = (refs[0], refs[1:]) if chained else (None, refs)
    attend_backward(
        t_ref, qkv_ref, zqk_ref, pm_ref, lse_ref, grad_ref, before_ref, *refs
    )


def attend_backward(
    t_ref, qkv_ref, zqk_ref, pm_ref, lse_ref, grad_ref, before_ref,
    grads_ref, after_ref,
    s_ref, d_ref, p_ref, ds_ref, gl_ref, high_ref, low_ref, gs_ref,
    key_ref, value_ref, zero_key_ref, zero_query_ref, carry_ref,
):
    t = t_ref[0]
    length = qkv_ref.shape[1]
    factor = HEAD_DIM ** -0.5
    upper = triangle(True)
    carry_ref[...] = jnp.zeros_like(carry_ref)
    key_ref[...] = jnp.zeros_like(key_ref)
    value_ref[...] = jnp.zeros_like(value_ref)
    zero_key_ref[...] = jnp.zeros_like(zero_key_ref)
    for tile in reversed(range(length // TILE)):
        start, span = window(tile)
        here = slice(tile * TILE, (tile + 1) * TILE)
        seen = slice(start, start + span)
        keys = qkv_ref[1, seen]
        values = qkv_ref[2, seen]
        queries = qkv_ref[0, here]
        grads = grad_ref[slot_rows(tile, t), :]
        queries_t = queries.astype(F32).T.astype(BF)
        grads_t = grads.astype(F32).T.astype(BF)
        query_grads = []
        for head in range(3):
            s_ref[head, :, :span] = dot_t(of_head(queries, head), with_head(keys, head))
            d_ref[head, :, :span] = dot_t(of_head(grads, head), with_head(values, head))
            clear_unseen(tile, p_ref.at[head])
            clear_unseen(tile, ds_ref.at[head])
            for row, first, last in chunks(tile, 16):
                rows = slice(row, row + 16)
                at = tile * TILE + row
                chances = jnp.exp(
                    s_ref[head, rows, first:last]
                    - pm_ref[at : at + 16, first:last]
                    - lse_ref[at : at + 16, head : head + 1]
                )
                p_ref[head, rows, first:last] = chances.astype(BF)
                product = chances * d_ref[head, rows, first:last]
                total = jnp.sum(product, axis=1, keepdims=True)
                grad = product - chances * total
                ds_ref[head, rows, first:last] = grad.astype(BF)
                if head == 0:
                    gl_ref[rows, first:last] = grad
                elif head == 1:
                    gl_ref[rows, first:last] += grad
                else:
                    grad = gl_ref[rows, first:last] + grad
                    gl_ref[rows, first:last] = grad
                    split_store(grad, high_ref, low_ref, rows, slice(first, last))
            own = slice(head * HEAD_DIM, (head + 1) * HEAD_DIM)
            value_ref[own, seen] += dot(grads_t[own], p_ref[head, :, :span])
            key_ref[own, seen] += dot(queries_t[own], ds_ref[head, :, :span])
            query_grads.append(dot(ds_ref[head, :, :span], with_head(keys, head)))
        pair, last_head = join_heads(query_grads)
        where = slot_rows(tile, t)
        grads_ref[0, where, : 2 * HEAD_DIM] = (pair * factor).astype(BF)
        grads_ref[0, where, 2 * HEAD_DIM :] = (last_head * factor).astype(BF)
        clear_unseen(tile, gl_ref)
        clear_unseen(tile, high_ref)
        clear_unseen(tile, low_ref)
        clear_unseen(tile, gs_ref)
        zero_queries = zqk_ref[0, here]
        zero_keys = zqk_ref[1, seen]
        inner = dot(upper, high_ref[:, :span]) + dot(upper, low_ref[:, :span])
        carry = carry_ref[:, seen]
        s_ref[0, :, :span] = inner + carry
        carry_ref[:, seen] = carry + inner[:1] + gl_ref[:1, :span]
        s_ref[1, :, :span] = dot_t(zero_queries, zero_keys)
        for row, first, last in chunks(tile, 16):
            rows = slice(row, row + 16)
            at = tile * TILE + row
            shape = (16, last - first)
            query = at + lax.broadcasted_iota(jnp.int32, shape, 0)
            key = start + first + lax.broadcasted_iota(jnp.int32, shape, 1)
            strict = (pm_ref[at : at + 16, first:last] < 0.5 * BIG) & (key < query)
            slope = jax.nn.sigmoid(s_ref[1, rows, first:last])
            gs_ref[rows, first:last] = jnp.where(
                strict, s_ref[0, rows, first:last] * slope * -SELECT_SCALE, 0.0
            ).astype(BF)
        zero_query_ref[here] = dot(gs_ref[:, :span], zero_keys) * factor
        zero_key_ref[:, seen] += dot(zero_queries.astype(F32).T.astype(BF), gs_ref[:, :span])
    for tile in range(length // TILE):
        here = slice(tile * TILE, (tile + 1) * TILE)
        where = slot_rows(tile, t)
        grads_ref[1, where, :] = key_ref[:, here].T.astype(BF)
        grads_ref[2, where, :] = value_ref[:, here].T.astype(BF)
        for c, share in enumerate((zero_query_ref[here], zero_key_ref[:, here].T)):
            if before_ref is not None:
                share = share + before_ref[c, where, :]
            after_ref[c, where, :] = share.astype(after_ref.dtype)


def gelu_and_slope(value):
    inner = GELU_A * (value + GELU_B * value * value * value)
    bend = jnp.tanh(inner)
    half = 0.5 * (1.0 + bend)
    slope = half + 0.5 * value * (1.0 - bend * bend) * (
        GELU_A * (1.0 + 3.0 * GELU_B * value * value)
    )
    return value * half, slope


def halves_of(own_ref, oth_ref, half, size):
    def pick(row):
        ref = own_ref if row < half else oth_ref
        return ref[row % half : row % half + size]

    return pick


def feed_kernel(
    x_own_ref, x_oth_ref, branch_ref, got_ref, gains_ref, biases_ref, cot_own_ref, cot_oth_ref,
    expand_hbm, shrink_hbm, far_hbm,
    middle_hbm, feed_hbm, feed_send_hbm, second_hbm, second_send_hbm, own_hbm, far_out_hbm,
    weights_ref, middle_ref, rows_ref, feed_ref, second_ref, feed_send_ref, second_send_ref,
    active_ref, hidden_ref, cot_ref, own_ref, far_ref, load_sem, store_sem,
):
    r = pl.program_id(0)
    length, width = rows_ref.shape
    half = length // 2
    units = active_ref.shape[1]
    loads = [
        pltpu.make_async_copy(source, weights_ref.at[i], load_sem.at[i])
        for i, source in enumerate((expand_hbm, shrink_hbm, far_hbm.at[0], far_hbm.at[1]))
    ]
    for load in loads:
        load.start()
    stores = []

    def store(source, target):
        copy = pltpu.make_async_copy(source, target.at[r], store_sem.at[len(stores)])
        copy.start()
        stores.append(copy)

    for row in range(0, length, HALF):
        here = slice(row, row + HALF)
        x_ref = x_own_ref if row < half else x_oth_ref
        there = (row + half) % length
        middle = (
            x_ref[row % half : row % half + HALF].astype(F32)
            + branch_ref[here]
            + got_ref[there : there + HALF].astype(F32)
        )
        middle_ref[here] = middle
        standard, _ = standardize(middle)
        rows_ref[here] = (standard * gains_ref[1:2] + biases_ref[1:2]).astype(BF)
    store(middle_ref, middle_hbm)
    cot_ref[:half] = cot_own_ref[...]
    cot_ref[half:] = cot_oth_ref[...]
    lower = ((0,), (0,))
    for quarter, grads_ref in enumerate((own_ref, far_ref)):
        expand_ref, shrink_ref = weights_ref.at[2 * quarter], weights_ref.at[2 * quarter + 1]
        loads[2 * quarter].wait()
        loads[2 * quarter + 1].wait()
        for row in range(0, length, TILE):
            here = slice(row, row + TILE)
            for unit in range(0, units, TILE):
                some = slice(unit, unit + TILE)
                active, slope = gelu_and_slope(dot(rows_ref[here], expand_ref[:, some]))
                active_ref[here, some] = active.astype(BF)
                hidden_ref[here, some] = (dot_t(cot_ref[here], shrink_ref[some]) * slope).astype(BF)
            feed = dot(active_ref[here], shrink_ref[...])
            second = dot_t(hidden_ref[here], expand_ref[...])
            if quarter == 1:
                feed = feed + feed_ref[here]
                second = second + second_ref[here]
                second_send_ref[here] = second.astype(BF)
                if row >= half:
                    feed_send_ref[row - half : row - half + TILE] = feed.astype(BF)
            feed_ref[here] = feed
            second_ref[here] = second
        if quarter == 1:
            store(second_ref, second_hbm)
            store(second_send_ref, second_send_hbm)
            store(feed_ref.at[:half], feed_hbm)
            store(feed_send_ref, feed_send_hbm)
        for unit in range(0, units, TILE):
            some = slice(unit, unit + TILE)
            grads_ref[0, some] = dot(hidden_ref[:, some], rows_ref[...], lower).astype(BF)
            grads_ref[1, some] = dot(active_ref[:, some], cot_ref[...], lower).astype(BF)
        store(grads_ref, own_hbm if quarter == 0 else far_out_hbm)
    for copy in stores:
        copy.wait()


def middle_kernel(
    t_ref, middle_ref, second_ref, got_ref, gains_ref, cot_own_ref, cot_oth_ref,
    own_ref, far_ref, att_own_ref, att_far_ref, *refs,
):
    grad_own_ref, to_own_ref, to_far_ref, out_own_ref, out_far_ref, sums_ref, branch_ref = refs
    length = middle_ref.shape[0]
    half = length // 2
    pick = halves_of(cot_own_ref, cot_oth_ref, half, WIDE)
    gain = bias = 0.0
    for row in range(0, length, WIDE):
        here = slice(row, row + WIDE)
        there = (row + half) % length
        grad = second_ref[here] + got_ref[there : there + WIDE].astype(F32)
        standard, scale = standardize(middle_ref[here])
        if row < half:
            gain = gain + jnp.sum(grad * standard, axis=0, keepdims=True)
            bias = bias + jnp.sum(grad, axis=0, keepdims=True)
        grad = pick(row).astype(F32) + norm_back(grad, standard, scale, gains_ref[1:2])
        if row < half:
            grad_own_ref[here] = grad
        branch = grad.astype(BF)
        branch_ref[here] = branch
        to_own_ref[here] = dot_t(branch, own_ref[...]).astype(BF)
        to_far_ref[here] = dot_t(branch, far_ref[...]).astype(BF)
    lower = ((0,), (0,))
    for ref in (to_own_ref, to_far_ref, grad_own_ref):
        complete(ref)
    out_own_ref[...] = dot(att_own_ref[...], branch_ref[...], lower).astype(BF)
    out_far_ref[...] = dot(att_far_ref[...], branch_ref[...], lower).astype(BF)
    sums_ref[0:1] = gain
    sums_ref[1:2] = bias


def first_back_kernel(
    rows_ref, grads_own_ref, grads_far_ref, grad_zero_ref, weight_own_ref, weight_far_ref,
    zero_ref, x_own_ref, x_oth_ref, out_own_ref, out_far_ref, feed_send_ref,
    handed_in_ref, first_ref, send_ref, own_ref, far_ref, sums_ref, handed_ref,
):
    length = rows_ref.shape[0]
    half = length // 2
    group = out_own_ref.shape[0]
    lower = ((0,), (0,))
    send_ref[0] = feed_send_ref[...]
    far_ref[:group] = dot(grads_far_ref[2], rows_ref[...], lower).astype(BF)
    far_ref[group:] = out_far_ref[...]
    own_ref[:group] = dot(grads_own_ref[2], rows_ref[...], lower).astype(BF)
    own_ref[group:] = out_own_ref[...]
    complete(far_ref)
    complete(own_ref)
    gain = bias = 0.0
    pick = halves_of(x_own_ref, x_oth_ref, half, TILE)
    for row in range(0, length, TILE):
        here = slice(row, row + TILE)
        first = 0.0
        for c in range(3):
            first = first + dot(grads_own_ref[c, here], weight_own_ref[c])
            first = first + dot(grads_far_ref[c, here], weight_far_ref[c])
        for c in range(2):
            first = first + dot(
                grad_zero_ref[c, here], zero_ref[c * HEAD_DIM : (c + 1) * HEAD_DIM]
            )
        standard, _ = standardize(pick(row).astype(F32))
        gain = gain + jnp.sum(first * standard, axis=0, keepdims=True)
        bias = bias + jnp.sum(first, axis=0, keepdims=True)
        if row < half:
            first_ref[here] = first
        else:
            send_ref[1, row - half : row - half + TILE] = first.astype(BF)
    sums_ref[0:1] = gain
    sums_ref[1:2] = bias


def early_kernel(
    t_ref, rows_ref, grads_own_ref, grads_far_ref, grad_zero_ref, zero_came_ref, small_ref, earlier_ref, *refs
):
    own_ref, far_ref, turned_ref = refs[1], refs[2], refs[-1]
    t = t_ref[0]
    length = rows_ref.shape[0]
    half = length // 2
    group = grads_own_ref.shape[2]
    for ref in (rows_ref, grad_zero_ref, zero_came_ref):
        ready(ref)
    for grads_ref, out_ref, place in ((grads_far_ref, far_ref, 2), (grads_own_ref, own_ref, 0)):
        for c in range(2):
            turned_ref[...] = grads_ref[c].astype(F32).T

            @pl.when(t == place)
            def _():
                for start in (0, half):
                    here = slice(start, start + half)
                    there = slice(half - start, length - start)
                    share = grad_zero_ref[c, here].astype(F32) + zero_came_ref[c, there].astype(F32)
                    turned_ref[:HEAD_DIM, here] += share.T

            out_ref[c * group : (c + 1) * group] = dot(
                turned_ref[...].astype(BF), rows_ref[...]
            ).astype(BF)
        if place == 2:
            out_ref[2 * group :] = small_ref[...]
        complete(out_ref)


VMEM_LIMIT = 56 * 1024 * 1024
SMEM = pl.BlockSpec(memory_space=pltpu.SMEM)
ANY = pl.BlockSpec(memory_space=pl.ANY)
COST = pl.CostEstimate(flops=10**6, bytes_accessed=10**4, transcendentals=0)


def scratch(*shape, dtype=F32):
    return pltpu.VMEM(shape, dtype)


class Fetched:
    def __init__(self, source, ref, sem):
        self.copy, self.ref, self.waited = pltpu.make_async_copy(source, ref, sem), ref, False
        self.shape = ref.shape
        self.copy.start()

    def ready(self):
        if not self.waited:
            self.copy.wait()
            self.waited = True
        return self.ref

    def __getitem__(self, index):
        return self.ready()[index]

    @property
    def at(self):
        return self.ready().at


def complete(ref):
    if isinstance(ref, Written):
        ref.finish()


def ready(ref):
    if isinstance(ref, Fetched):
        ref.ready()


class Written:
    def __init__(self, target, ref, sem):
        self.copy, self.ref, self.sent = pltpu.make_async_copy(ref, target, sem), ref, False
        self.shape, self.dtype = ref.shape, ref.dtype

    def __getitem__(self, index):
        return self.ref[index]

    def __setitem__(self, index, value):
        self.ref[index] = value

    @property
    def at(self):
        return self.ref.at

    def finish(self):
        if not self.sent:
            self.copy.start()
            self.sent = True


def staged_kernel(kernel, kinds, staged_outs, extra, *refs):
    r = pl.program_id(0)
    count, handed = len(kinds), extra[0]
    ins, rest = refs[:count], refs[count:]
    handed_in, rest = rest[:handed], rest[handed:]
    outs, rest = rest[: extra[1]], rest[extra[1] :]
    handed_out, rest = rest[:handed], rest[handed:]
    plain, buffers = rest[: extra[2]], list(rest[extra[2] :])
    sem = buffers.pop()
    arguments, used = [], 0
    sources = {"row": lambda v: v.at[r], "whole": lambda v: v, "out": lambda v: v.at[3]}
    for kind, ref in zip(kinds, ins):
        if kind in sources:
            ref = Fetched(sources[kind](ref), buffers.pop(0), sem.at[used])
            used += 1
        arguments.append(ref)
    results = []
    for ref, big in zip(outs, staged_outs):
        if big:
            ref = Written(ref.at[r], buffers.pop(0), sem.at[used])
            used += 1
        results.append(ref)
    kernel(*arguments, *handed_in, *results, *handed_out, *plain)
    for ref in arguments:
        if isinstance(ref, Fetched):
            ref.ready()
    for ref in results:
        complete(ref)
    for ref in results:
        if isinstance(ref, Written):
            ref.copy.wait()


def whole(shape):
    return pl.BlockSpec(shape, lambda r: (0,) * len(shape))


def by_row(shape):
    return pl.BlockSpec((None,) + shape[1:], lambda r: (r,) + (0,) * (len(shape) - 1))


def third(shape):
    return pl.BlockSpec((None,) + shape[1:], lambda r: (3,) + (0,) * (len(shape) - 1))


def call(
    kernel, n, operands, outs, scratches, handed=(), placed=None, staged=True, cost=None
):
    arrays = [v for _, v in operands] + list(handed)
    kinds = [
        "block" if v.size < 2**16 or not staged else kind if kind != "block" else kind
        for kind, v in operands
    ]
    kinds = [old if old in ("smem", "any") else new for (old, _), new in zip(operands, kinds)]
    part = {"row": lambda s: s[1:], "whole": lambda s: s, "out": lambda s: s[1:]}
    buffers = [
        scratch(*part[k](v.shape), dtype=v.dtype) for k, (_, v) in zip(kinds, operands) if k in part
    ]
    big = [staged and placed is None and s[-2] >= 16 for s, _ in outs]
    buffers += [scratch(*s, dtype=d) for (s, d), b in zip(outs, big) if b]
    places = {"row": by_row, "whole": whole, "out": third}
    specs = [
        SMEM if old == "smem" else places[old](v.shape) if k == "block" else ANY
        for k, (old, v) in zip(kinds, operands)
    ]
    return pl.pallas_call(
        partial(staged_kernel, kernel, kinds, big, (len(handed), len(outs), len(scratches))),
        grid=(n,),
        in_specs=specs + [ANY] * len(handed),
        out_specs=[
            ANY if b or placed is not None else by_row((n,) + s) for (s, _), b in zip(outs, big)
        ]
        + [ANY] * len(handed),
        out_shape=[jax.ShapeDtypeStruct((n,) + s, d) for s, d in outs]
        + [jax.ShapeDtypeStruct(v.shape, v.dtype) for v in handed],
        scratch_shapes=scratches + buffers + [pltpu.SemaphoreType.DMA((max(len(buffers), 1),))],
        input_output_aliases={len(operands) + i: len(outs) + i for i in range(len(handed))},
        compiler_params=pltpu.CompilerParams(vmem_limit_bytes=VMEM_LIMIT),
        cost_estimate=cost or COST,
    )(*arrays)


def idle_kernel(*refs):
    del refs


def after(value, *earlier):
    return pl.pallas_call(
        idle_kernel,
        in_specs=[ANY] * (1 + len(earlier)),
        out_specs=ANY,
        out_shape=jax.ShapeDtypeStruct(value.shape, value.dtype),
        input_output_aliases={0: 0},
        cost_estimate=COST,
    )(value, *earlier)


def attend_first(t, x_own, x_oth, gains, biases, weight, segments):
    n, _, width = x_own.shape
    length, group, span = segments.shape[1], weight.shape[1], (REACH + 1) * TILE
    return call(
        first_kernel,
        n,
        [
            ("smem", t),
            ("row", x_own),
            ("row", x_oth),
            ("whole", gains),
            ("whole", biases),
            ("whole", weight),
            ("row", segments.astype(F32)[:, None, :]),
        ],
        [
            ((length, width), BF),
            ((3, length, group), BF),
            ((2, length, HEAD_DIM), BF),
            ((length, span), F32),
            ((length, group), BF),
            ((length, 128), F32),
            ((1, 128), F32),
            ((2 * HEAD_DIM, width), BF),
        ],
        [
            scratch(3, TILE, span),
            scratch(3, TILE, span, dtype=BF),
            scratch(TILE, span, dtype=BF),
            scratch(TILE, span, dtype=BF),
            scratch(1, length),
            scratch(length, 8),
        ],
        staged=False,
    )


def attend_second(t, rows, weight_own, weight_far, pm, att_own):
    n, length, width = rows.shape
    group, span = weight_far.shape[1], pm.shape[2]
    return call(
        second_kernel,
        n,
        [
            ("smem", t),
            ("row", rows),
            ("whole", weight_own),
            ("whole", weight_far),
            ("row", pm),
            ("row", att_own),
        ],
        [
            ((3, length, group), BF),
            ((length, group), BF),
            ((length, 128), F32),
            ((length, width), F32),
            ((length, width), BF),
        ],
        [scratch(3, TILE, span), scratch(3, TILE, span, dtype=BF)],
        staged=False,
    )


def attend_back(t, qkv, zqk, pm, lse, grad, before=None):
    n, _, length, group = qkv.shape
    span = pm.shape[2]
    operands = [("smem", t)] + [("row", v) for v in (qkv, zqk, pm, lse, grad)]
    if before is not None:
        operands.append(("row", before))
    return call(
        partial(backward_kernel, before is not None),
        n,
        operands,
        [
            ((3, length, group), BF),
            ((2, length, HEAD_DIM), F32 if before is None else BF),
        ],
        [
            scratch(3, TILE, span),
            scratch(3, TILE, span),
            scratch(3, TILE, span, dtype=BF),
            scratch(3, TILE, span, dtype=BF),
            scratch(TILE, span),
            scratch(TILE, span, dtype=BF),
            scratch(TILE, span, dtype=BF),
            scratch(TILE, span, dtype=BF),
            scratch(group, length),
            scratch(group, length),
            scratch(HEAD_DIM, length),
            scratch(length, HEAD_DIM),
            scratch(1, length),
        ],
        staged=False,
    )


def feed_forward(x_own, x_oth, branch, got, gains, biases, cot_own, cot_oth, expand, shrink, far):
    n, length, width = branch.shape
    units = expand.shape[1]
    half = length // 2
    return call(
        feed_kernel,
        n,
        [("row", v) for v in (x_own, x_oth, branch, got)]
        + [("whole", gains), ("whole", biases), ("row", cot_own), ("row", cot_oth)]
        + [("any", expand), ("any", shrink), ("any", far)],
        [
            ((length, width), F32),
            ((half, width), F32),
            ((half, width), BF),
            ((length, width), F32),
            ((length, width), BF),
            ((2, units, width), BF),
            ((2, units, width), BF),
        ],
        [
            scratch(4, units, width, dtype=BF),
            scratch(length, width),
            scratch(length, width, dtype=BF),
            scratch(length, width),
            scratch(length, width),
            scratch(half, width, dtype=BF),
            scratch(length, width, dtype=BF),
            scratch(length, units, dtype=BF),
            scratch(length, units, dtype=BF),
            scratch(length, width, dtype=BF),
            scratch(2, units, width, dtype=BF),
            scratch(2, units, width, dtype=BF),
            pltpu.SemaphoreType.DMA((4,)),
            pltpu.SemaphoreType.DMA((7,)),
        ],
        placed=ANY,
        staged=False,
    )


def middle_back(t, middle, second, got, gains, cot_own, cot_oth, weight_own, weight_far, att_own, att_far):
    n, length, width = middle.shape
    group = weight_far.shape[1]
    return call(
        middle_kernel,
        n,
        [
            ("smem", t),
            ("row", middle),
            ("row", second),
            ("row", got),
            ("whole", gains),
            ("row", cot_own),
            ("row", cot_oth),
            ("whole", weight_own),
            ("out", weight_far),
            ("row", att_own),
            ("row", att_far),
        ],
        [
            ((length // 2, width), F32),
            ((length, group), BF),
            ((length, group), BF),
            ((group, width), BF),
            ((group, width), BF),
            ((2, width), F32),
        ],
        [scratch(length, width, dtype=BF)],
        staged=False,
    )


def first_back(
    rows, grads_own, grads_far, grad_zero, weight_own, weight_far, zero,
    x_own, x_oth, out_own, out_far, feed_send, handed,
):
    n, length, width = rows.shape
    group = weight_far.shape[1]
    return call(
        first_back_kernel,
        n,
        [
            ("row", rows),
            ("row", grads_own),
            ("row", grads_far),
            ("row", grad_zero),
            ("whole", weight_own),
            ("whole", weight_far),
            ("whole", zero),
            ("row", x_own),
            ("row", x_oth),
            ("row", out_own),
            ("row", out_far),
            ("row", feed_send),
        ],
        [
            ((length // 2, width), F32),
            ((2, length // 2, width), BF),
            ((2 * group, width), BF),
            ((2 * group, width), BF),
            ((2, width), F32),
        ],
        [],
        (handed,),
        staged=False,
    )


def early_products(t, rows, grads_own, grads_far, grad_zero, zero_came, small, earlier, handed):
    n, length, width = rows.shape
    group = grads_own.shape[3]
    return call(
        early_kernel,
        n,
        [
            ("smem", t),
            ("row", rows),
            ("row", grads_own),
            ("row", grads_far),
            ("row", grad_zero),
            ("row", zero_came),
            ("row", small),
            ("any", earlier),
        ],
        [((2 * group, width), BF), ((2 * group + small.shape[1], width), BF)],
        [scratch(group, length)],
        handed,
        staged=False,
        cost=pl.CostEstimate(
            flops=4 * 10**9, bytes_accessed=24 * 10**6, transcendentals=0
        ),
    )


def per_device(
    layer_input,
    cotangent,
    segment_ids,
    norm_gains,
    norm_biases,
    attend_weight,
    output_weight,
    expand_weight,
    shrink_weight,
):
    t = lax.axis_index("tensor")
    chip = t // 2
    core = t % 2
    rows, block, width = layer_input.shape
    n = rows // 2
    length = segment_ids.shape[1]
    half = length // 2
    units = expand_weight.shape[1]
    size, dp = lax.axis_size("tensor"), lax.axis_size("dp")
    across = [(i, i ^ 2) for i in range(size)]
    beside = [(i, i ^ 1) for i in range(size)]
    pairs = [[i, i ^ 2] for i in range(size) if i < i ^ 2]

    def swap_chip(v):
        return lax.ppermute(v, "tensor", across)

    def swap_core(v):
        return lax.ppermute(v, "tensor", beside)

    def mine(v):
        return lax.dynamic_slice_in_dim(v, chip * n, n, 0)

    def theirs(v):
        return lax.dynamic_slice_in_dim(v, (1 - chip) * n, n, 0)

    zero_own = attend_weight[:2, :, :HEAD_DIM].transpose(0, 2, 1).reshape(2 * HEAD_DIM, width)
    zero_low = jnp.where(chip == 0, zero_own, lax.ppermute(zero_own, "tensor", [(0, 2)]))
    zero_low = jnp.broadcast_to(zero_low, (n, *zero_low.shape))
    x_own = jnp.concatenate(
        [mine(layer_input), swap_chip(theirs(layer_input)), zero_low], axis=1
    )
    x_oth = swap_core(x_own)
    index = lax.axis_index("dp")
    cut = units // dp
    pieces = jnp.stack(
        [lax.dynamic_slice_in_dim(v, index * cut, cut, 0) for v in (expand_weight, shrink_weight)]
    )
    far_feed = lax.all_gather(after(swap_chip(pieces), x_own), "dp", axis=1, tiled=True)
    group = output_weight.shape[0]
    attend_own = attend_weight.transpose(0, 2, 1)
    weight_far = swap_chip(
        jnp.concatenate([attend_own, output_weight.reshape(1, group, width)])
    )
    segments = mine(segment_ids)

    t_array = t.reshape(1)
    first_rows, qkv_own, zqk, pm, att_own, lse_own, kept, zero_weight = attend_first(
        t_array, x_own, x_oth, norm_gains, norm_biases, attend_own, segments
    )
    zero_weight = zero_weight[0]
    cot_came = swap_chip(after(theirs(cotangent), first_rows))
    cot_own = jnp.concatenate([mine(cotangent), cot_came], axis=1)
    cot_oth = swap_core(cot_own)
    qkv_far, att_far, lse_far, branch, branch_send = attend_second(
        t_array, first_rows, output_weight, weight_far, pm, att_own
    )
    middle, feed, feed_send, second, second_send, feed_grads_own, feed_grads_far = feed_forward(
        x_own, x_oth, branch, swap_core(after(branch_send, cot_own)), norm_gains, norm_biases,
        cot_own, cot_oth, expand_weight, shrink_weight, far_feed,
    )

    def over_rows(v):
        return v[0] if n == 1 else jnp.sum(v.astype(F32), axis=0).astype(BF)

    second_came = swap_core(second_send)
    feed_grads_came = swap_chip(over_rows(feed_grads_far))
    grad_middle, to_own, to_far, out_own, out_far, sums_second = middle_back(
        t_array, middle, second, second_came, norm_gains, cot_own, cot_oth,
        output_weight, weight_far, att_own, att_far,
    )

    def total(a, b):
        return (a.astype(F32) + b.astype(F32)).astype(BF)

    def packed(small):
        high = small.astype(BF)
        low = (small - high.astype(F32)).astype(BF)
        both = jnp.concatenate([high, low])
        return jnp.pad(both, ((0, 16 - both.shape[0]), (0, 0)))

    def unpacked(both):
        return both[:5].astype(F32) + both[5:10].astype(F32)

    def over_dp(v, small=None, order=(), wait=None, noted=None, sends=None):
        steps = [1 << k for k in range(dp.bit_length() - 1)]
        steps = [k for k in order if k in steps] + [k for k in steps if k not in order]
        for step in steps:
            upper = (index // step) % 2
            part = v.shape[0] // 2
            keep = lax.dynamic_slice_in_dim(v, upper * part, part, 0)
            send = lax.dynamic_slice_in_dim(v, (1 - upper) * part, part, 0)
            if small is not None:
                send = jnp.concatenate([send, packed(small)])
            if sends is not None:
                sends.append(send)
            came = lax.ppermute(send, "dp", [(i, i ^ step) for i in range(dp)])
            v = total(keep, came[:part])
            if sends is not None:
                sums.append(v)
            if small is not None:
                small = small + unpacked(came[part:])
        for step in reversed(steps):
            upper = (index // step) % 2
            if wait is not None and step == steps[0]:
                v = after(v, wait)
            if noted is not None:
                noted.append(v)
            came = lax.ppermute(v, "dp", [(i, i ^ step) for i in range(dp)])
            if noted is not None and step == steps[0]:
                v = jnp.where(upper == 0, v, came), jnp.where(upper == 0, came, v)
            else:
                v = jnp.where(upper == 0, jnp.concatenate([v, came]), jnp.concatenate([came, v]))
        return v, small

    grads_far, zero_far = attend_back(t_array, qkv_far, zqk, pm, lse_far, to_far)
    grads_own, grad_zero = attend_back(t_array, qkv_own, zqk, pm, lse_own, to_own, zero_far)
    zero_came = lax.ppermute(grad_zero, "tensor", [(1, 0), (3, 2)])
    first, first_send, own_late, far_late, sums_first, feed_grads_own = first_back(
        first_rows, grads_own, grads_far, grad_zero, attend_own, weight_far, zero_weight,
        x_own, x_oth, out_own, out_far, feed_send, feed_grads_own,
    )
    feed_grads_own = over_rows(feed_grads_own)
    feed_sums = [total(feed_grads_own[i], feed_grads_came[i]) for i in range(2)]
    sends, sums = [], []
    grad_expand, _ = over_dp(feed_sums[0], None, (), None, None, sends)
    far_late = over_rows(far_late)
    late_came = swap_chip(far_late)
    sums_first, sums_second = jnp.sum(sums_first, axis=0), jnp.sum(sums_second, axis=0)
    small = jnp.stack(
        [
            sums_first[0],
            sums_second[0],
            sums_first[1],
            sums_second[1],
            jnp.full((width,), 0.5 * jnp.sum(kept[:, 0, 0]), F32),
        ]
    )
    small_rows = jnp.broadcast_to(packed(small), (n, 16, width))
    own_early, far_early, own_late = early_products(
        t_array, after(first_rows, far_late), grads_own, grads_far, grad_zero, zero_came, small_rows,
        sends[0], (own_late,),
    )
    came = swap_core(first_send)
    came = after(came, sums[min(1, len(sums) - 1)]).astype(F32)
    far_early = (
        far_early[0]
        if n == 1
        else jnp.concatenate([over_rows(far_early[:, : 2 * group]), packed(small)])
    )
    early_came = swap_chip(far_early)
    small = small + unpacked(early_came[2 * group :])
    proj = jnp.concatenate(
        [
            total(over_rows(own_early), early_came[: 2 * group]),
            total(over_rows(own_late), late_came),
        ]
    )
    noted = []
    (grad_early, grad_late), small = over_dp(proj, small, (), None, noted)
    small = small + swap_core(small)
    grad_shrink, _ = over_dp(feed_sums[1], None, (2, 1), noted[max(len(noted) - 2, 0)])

    layer_own = (middle[:, :half] + feed + came[:, 0]).astype(BF)
    standard_first, scale_first = standardize(x_own[:, :half].astype(F32))
    input_part = norm_back(first + came[:, 1], standard_first, scale_first, norm_gains[0])
    input_own = (grad_middle + input_part).astype(BF)
    results = jnp.stack([layer_own, input_own])
    home = swap_chip(results[:, :, block:])
    stays = results[:, :, :block]
    low, high = jnp.where(chip == 0, stays, home), jnp.where(chip == 0, home, stays)
    results = jnp.concatenate([low, high], axis=1)
    grad_attend = jnp.concatenate([grad_early, grad_late[:group]]).astype(F32)
    grad_attend = grad_attend.reshape(3, group, width).transpose(0, 2, 1)
    grad_output = grad_late[group:].astype(F32)
    kept_fraction = small[4, 0] / (rows * length * dp)
    return (
        results[0],
        results[1],
        small[:2],
        small[2:4],
        grad_attend,
        grad_output,
        grad_expand.astype(F32).T,
        grad_shrink.astype(F32),
        kept_fraction,
    )


def solution(mesh):
    return jax.shard_map(
        per_device,
        mesh=mesh,
        in_specs=(
            P("dp", "tensor", None),
            P("dp", "tensor", None),
            P("dp", None),
            P(),
            P(),
            P(None, None, "tensor"),
            P("tensor", None),
            P(None, "tensor"),
            P("tensor", None),
        ),
        out_specs=(
            P("dp", "tensor", None),
            P("dp", "tensor", None),
            P(),
            P(),
            P(None, None, "tensor"),
            P("tensor", None),
            P(None, "tensor"),
            P("tensor", None),
            P(),
        ),
        check_vma=False,
    )
```

```python
from functools import partial

import jax
import jax.numpy as jnp
from jax import lax
from jax.experimental import pallas as pl
from jax.experimental.pallas import tpu as pltpu
from jax.sharding import PartitionSpec as P

HEAD_DIM = 64
EPSILON = 1e-05
SELECT_SCALE = 0.02
THRESHOLD = 4.0
GELU_A = 0.7978845608028654
GELU_B = 0.044715
BF = jnp.bfloat16
F32 = jnp.float32


def mm(spec, a, b):
    return jnp.einsum(spec, a, b, preferred_element_type=F32)


def standardize(values):
    average = jnp.mean(values, axis=-1, keepdims=True)
    centred = values - average
    variance = jnp.mean(centred * centred, axis=-1, keepdims=True)
    scale = lax.rsqrt(variance + EPSILON)
    return centred * scale, scale


def norm_back(grad, standard, scale, gains):
    inner = grad * gains
    return scale * (
        inner
        - jnp.mean(inner, axis=-1, keepdims=True)
        - standard * jnp.mean(inner * standard, axis=-1, keepdims=True)
    )


TILE = 256
WIDE = 512
HALF = 128
CHUNK = 32
REACH = 2
BIG = 1e30


def dot(a, b, dims=((1,), (0,))):
    return lax.dot_general(a, b, (dims, ((), ())), preferred_element_type=F32)


def dot_t(a, b):
    return dot(a, b, ((1,), (1,)))


def window(tile):
    start = max(0, tile - REACH) * TILE
    return start, (tile + 1) * TILE - start


def half_columns(tile, half):
    start, span = window(tile)
    first = max(0, tile * TILE + half * HALF - REACH * TILE) - start
    return first, span - HALF if half == 0 else span


def chunks(tile, size=CHUNK):
    for half in range(2):
        first, last = half_columns(tile, half)
        for row in range(half * HALF, (half + 1) * HALF, size):
            yield row, first, last


def clear_unseen(tile, ref):
    start, span = window(tile)
    for half in range(2):
        first, last = half_columns(tile, half)
        rows = slice(half * HALF, (half + 1) * HALF)
        if first > 0:
            ref[rows, :first] = jnp.zeros((HALF, first), ref.dtype)
        if last < span:
            ref[rows, last:span] = jnp.zeros((HALF, span - last), ref.dtype)


def flip(v):
    return ((v & 1) << 1) | (v >> 1)


def slot_rows(block, t):
    return pl.ds(pl.multiple_of(flip(block ^ t) * TILE, TILE), TILE)


def block_rows(slot, t):
    return pl.ds(pl.multiple_of((flip(slot) ^ t) * TILE, TILE), TILE)


def lane_mask(shape, head):
    lanes = lax.broadcasted_iota(jnp.int32, shape, 1)
    return lanes < HEAD_DIM if head == 0 else lanes >= HEAD_DIM


def of_head(value, head):
    if head == 2:
        return value[:, 2 * HEAD_DIM :]
    pair = value[:, : 2 * HEAD_DIM]
    return jnp.where(lane_mask(pair.shape, head), pair, jnp.zeros_like(pair))


def with_head(value, head):
    return value[:, 2 * HEAD_DIM :] if head == 2 else value[:, : 2 * HEAD_DIM]


def join_heads(parts):
    pair = jnp.where(lane_mask(parts[0].shape, 0), parts[0], parts[1])
    return pair, parts[2]


def triangle(upper):
    rows = lax.broadcasted_iota(jnp.int32, (TILE, TILE), 0)
    columns = lax.broadcasted_iota(jnp.int32, (TILE, TILE), 1)
    inside = columns > rows if upper else columns < rows
    return inside.astype(F32).astype(BF)


def split_store(value, high_ref, low_ref, rows, columns):
    high = value.astype(BF)
    high_ref[rows, columns] = high
    low_ref[rows, columns] = (value - high.astype(F32)).astype(BF)


def place(t, result, out_ref, c):
    if c == 0:
        result = result.astype(BF).astype(F32) * (HEAD_DIM ** -0.5)
    result = result.astype(BF)
    for slot in range(result.shape[0] // TILE):
        out_ref[c, block_rows(slot, t), :] = result[slot * TILE : (slot + 1) * TILE]


def project(t, rows_ref, weight_ref, out_ref):
    for c in range(3):
        place(t, dot_t(rows_ref[...], weight_ref[c]), out_ref, c)


def attend_group(t, qkv_ref, pm_ref, att_ref, lse_ref, s_ref, p_ref, size):
    length = qkv_ref.shape[1]
    for tile in range(length // TILE):
        start, span = window(tile)
        here = slice(tile * TILE, (tile + 1) * TILE)
        keys = qkv_ref[1, start : start + span]
        values = qkv_ref[2, start : start + span]
        queries = qkv_ref[0, here]
        outs = []
        for head in range(3):
            s_ref[head, :, :span] = dot_t(of_head(queries, head), with_head(keys, head))
            clear_unseen(tile, p_ref.at[head])
            for row, first, last in chunks(tile, size):
                rows = slice(row, row + size)
                logits = (
                    s_ref[head, rows, first:last]
                    - pm_ref[tile * TILE + row : tile * TILE + row + size, first:last]
                )
                highest = jnp.max(logits, axis=1, keepdims=True)
                powers = jnp.exp(logits - highest)
                total = jnp.sum(powers, axis=1, keepdims=True)
                p_ref[head, rows, first:last] = (powers * (1.0 / total)).astype(BF)
                lse_ref[tile * TILE + row : tile * TILE + row + size, head : head + 1] = (
                    highest + jnp.log(total)
                )
            outs.append(dot(p_ref[head, :, :span], with_head(values, head)))
        pair, last_head = join_heads(outs)
        where = slot_rows(tile, t)
        att_ref[where, : 2 * HEAD_DIM] = pair.astype(BF)
        att_ref[where, 2 * HEAD_DIM :] = last_head.astype(BF)


def first_kernel(
    t_ref, x_own_ref, x_oth_ref, gains_ref, biases_ref, weight_ref, seg_ref,
    rows_ref, qkv_ref, zqk_ref, pm_ref, att_ref, lse_ref, kept_ref, zero_ref,
    s_ref, p_ref, high_ref, low_ref, carry_ref, seg_col_ref,
):
    t = t_ref[0]
    length = rows_ref.shape[0]
    half = length // 2
    for part, ref in enumerate((x_own_ref, x_oth_ref)):
        for row in range(0, half, HALF):
            standard, _ = standardize(ref[row : row + HALF].astype(F32))
            rows_ref[part * half + row : part * half + row + HALF] = (
                standard * gains_ref[0:1] + biases_ref[0:1]
            ).astype(BF)
    zero_ref[...] = jnp.where(t % 2 == 0, x_own_ref[half:], x_oth_ref[half:])
    for c in range(2):
        weight = zero_ref[c * HEAD_DIM : (c + 1) * HEAD_DIM]
        place(t, dot_t(rows_ref[...], weight), zqk_ref, c)
    project(t, rows_ref, weight_ref, qkv_ref)
    for ref in (rows_ref, zqk_ref, qkv_ref, zero_ref):
        complete(ref)
    for tile in range(length // TILE):
        here = slice(tile * TILE, (tile + 1) * TILE)
        seg_col_ref[here] = jnp.broadcast_to(seg_ref[:, here], (8, TILE)).T
    lower = triangle(False)
    carry_ref[...] = jnp.zeros_like(carry_ref)
    for tile in range(length // TILE):
        start, span = window(tile)
        s_ref[0, :, :span] = dot_t(
            zqk_ref[0, tile * TILE : (tile + 1) * TILE], zqk_ref[1, start : start + span]
        )
        clear_unseen(tile, high_ref)
        clear_unseen(tile, low_ref)
        last_row = None
        for row, first, last in chunks(tile):
            rows = slice(row, row + CHUNK)
            select = s_ref[0, rows, first:last]
            soft = jnp.maximum(select, 0.0) + jnp.log1p(jnp.exp(-jnp.abs(select)))
            at = tile * TILE + row
            query = at + lax.broadcasted_iota(jnp.int32, select.shape, 0)
            key = start + first + lax.broadcasted_iota(jnp.int32, select.shape, 1)
            same = seg_col_ref[at : at + CHUNK, :1] == seg_ref[:, start + first : start + last]
            chosen = jnp.where(same & (key < query), SELECT_SCALE * soft, 0.0)
            split_store(chosen, high_ref, low_ref, rows, slice(first, last))
            last_row = chosen[CHUNK - 1 :]
        carry = carry_ref[:, start : start + span]
        inner = dot(lower, high_ref[:, :span]) + dot(lower, low_ref[:, :span])
        s_ref[1, :, :span] = inner + carry
        carry_ref[:, start : start + span] = carry + inner[TILE - 1 :]
        carry_ref[:, start + first : start + last] += last_row
        for row, first, last in chunks(tile):
            rows = slice(row, row + CHUNK)
            at = tile * TILE + row
            shape = (CHUNK, last - first)
            query = at + lax.broadcasted_iota(jnp.int32, shape, 0)
            key = start + first + lax.broadcasted_iota(jnp.int32, shape, 1)
            same = seg_col_ref[at : at + CHUNK, :1] == seg_ref[:, start + first : start + last]
            pm_ref[at : at + CHUNK, first:last] = jnp.where(
                same & (key <= query), s_ref[1, rows, first:last], BIG
            )
    kept = jnp.sum(jax.nn.sigmoid(carry_ref[...] - THRESHOLD), axis=1, keepdims=True)
    kept_ref[...] = jnp.broadcast_to(kept, kept_ref.shape)
    complete(pm_ref)
    attend_group(t, qkv_ref, pm_ref, att_ref, lse_ref, s_ref, p_ref, 16)


def second_kernel(
    t_ref, rows_ref, own_ref, far_ref, pm_ref, att_own_ref,
    qkv_ref, att_ref, lse_ref, branch_ref, send_ref,
    s_ref, p_ref,
):
    t = t_ref[0]
    project(t, rows_ref, far_ref, qkv_ref)
    complete(qkv_ref)
    attend_group(t, qkv_ref, pm_ref, att_ref, lse_ref, s_ref, p_ref, 64)
    complete(att_ref)
    complete(lse_ref)
    for row in range(0, rows_ref.shape[0], TILE):
        here = slice(row, row + TILE)
        branch = dot(att_own_ref[here], own_ref[...]) + dot(
            att_ref[here], far_ref[3]
        )
        branch_ref[here] = branch
        send_ref[here] = branch.astype(BF)


def backward_kernel(
    chained, t_ref, qkv_ref, zqk_ref, pm_ref, lse_ref, grad_ref, *refs
):
    before_ref, refs = (refs[0], refs[1:]) if chained else (None, refs)
    attend_backward(
        t_ref, qkv_ref, zqk_ref, pm_ref, lse_ref, grad_ref, before_ref, *refs
    )


def attend_backward(
    t_ref, qkv_ref, zqk_ref, pm_ref, lse_ref, grad_ref, before_ref,
    grads_ref, after_ref,
    s_ref, d_ref, p_ref, ds_ref, gl_ref, high_ref, low_ref, gs_ref,
    key_ref, value_ref, zero_key_ref, zero_query_ref, carry_ref,
):
    t = t_ref[0]
    length = qkv_ref.shape[1]
    factor = HEAD_DIM ** -0.5
    upper = triangle(True)
    carry_ref[...] = jnp.zeros_like(carry_ref)
    key_ref[...] = jnp.zeros_like(key_ref)
    value_ref[...] = jnp.zeros_like(value_ref)
    zero_key_ref[...] = jnp.zeros_like(zero_key_ref)
    for tile in reversed(range(length // TILE)):
        start, span = window(tile)
        here = slice(tile * TILE, (tile + 1) * TILE)
        seen = slice(start, start + span)
        keys = qkv_ref[1, seen]
        values = qkv_ref[2, seen]
        queries = qkv_ref[0, here]
        grads = grad_ref[slot_rows(tile, t), :]
        queries_t = queries.astype(F32).T.astype(BF)
        grads_t = grads.astype(F32).T.astype(BF)
        query_grads = []
        for head in range(3):
            s_ref[head, :, :span] = dot_t(of_head(queries, head), with_head(keys, head))
            d_ref[head, :, :span] = dot_t(of_head(grads, head), with_head(values, head))
            clear_unseen(tile, p_ref.at[head])
            clear_unseen(tile, ds_ref.at[head])
            for row, first, last in chunks(tile, 16):
                rows = slice(row, row + 16)
                at = tile * TILE + row
                chances = jnp.exp(
                    s_ref[head, rows, first:last]
                    - pm_ref[at : at + 16, first:last]
                    - lse_ref[at : at + 16, head : head + 1]
                )
                p_ref[head, rows, first:last] = chances.astype(BF)
                product = chances * d_ref[head, rows, first:last]
                total = jnp.sum(product, axis=1, keepdims=True)
                grad = product - chances * total
                ds_ref[head, rows, first:last] = grad.astype(BF)
                if head == 0:
                    gl_ref[rows, first:last] = grad
                elif head == 1:
                    gl_ref[rows, first:last] += grad
                else:
                    grad = gl_ref[rows, first:last] + grad
                    gl_ref[rows, first:last] = grad
                    split_store(grad, high_ref, low_ref, rows, slice(first, last))
            own = slice(head * HEAD_DIM, (head + 1) * HEAD_DIM)
            value_ref[own, seen] += dot(grads_t[own], p_ref[head, :, :span])
            key_ref[own, seen] += dot(queries_t[own], ds_ref[head, :, :span])
            query_grads.append(dot(ds_ref[head, :, :span], with_head(keys, head)))
        pair, last_head = join_heads(query_grads)
        where = slot_rows(tile, t)
        grads_ref[0, where, : 2 * HEAD_DIM] = (pair * factor).astype(BF)
        grads_ref[0, where, 2 * HEAD_DIM :] = (last_head * factor).astype(BF)
        clear_unseen(tile, gl_ref)
        clear_unseen(tile, high_ref)
        clear_unseen(tile, low_ref)
        clear_unseen(tile, gs_ref)
        zero_queries = zqk_ref[0, here]
        zero_keys = zqk_ref[1, seen]
        inner = dot(upper, high_ref[:, :span]) + dot(upper, low_ref[:, :span])
        carry = carry_ref[:, seen]
        s_ref[0, :, :span] = inner + carry
        carry_ref[:, seen] = carry + inner[:1] + gl_ref[:1, :span]
        s_ref[1, :, :span] = dot_t(zero_queries, zero_keys)
        for row, first, last in chunks(tile, 16):
            rows = slice(row, row + 16)
            at = tile * TILE + row
            shape = (16, last - first)
            query = at + lax.broadcasted_iota(jnp.int32, shape, 0)
            key = start + first + lax.broadcasted_iota(jnp.int32, shape, 1)
            strict = (pm_ref[at : at + 16, first:last] < 0.5 * BIG) & (key < query)
            slope = jax.nn.sigmoid(s_ref[1, rows, first:last])
            gs_ref[rows, first:last] = jnp.where(
                strict, s_ref[0, rows, first:last] * slope * -SELECT_SCALE, 0.0
            ).astype(BF)
        zero_query_ref[here] = dot(gs_ref[:, :span], zero_keys) * factor
        zero_key_ref[:, seen] += dot(zero_queries.astype(F32).T.astype(BF), gs_ref[:, :span])
    for tile in range(length // TILE):
        here = slice(tile * TILE, (tile + 1) * TILE)
        where = slot_rows(tile, t)
        grads_ref[1, where, :] = key_ref[:, here].T.astype(BF)
        grads_ref[2, where, :] = value_ref[:, here].T.astype(BF)
        for c, share in enumerate((zero_query_ref[here], zero_key_ref[:, here].T)):
            if before_ref is not None:
                share = share + before_ref[c, where, :]
            after_ref[c, where, :] = share.astype(after_ref.dtype)


def gelu_and_slope(value):
    inner = GELU_A * (value + GELU_B * value * value * value)
    bend = jnp.tanh(inner)
    half = 0.5 * (1.0 + bend)
    slope = half + 0.5 * value * (1.0 - bend * bend) * (
        GELU_A * (1.0 + 3.0 * GELU_B * value * value)
    )
    return value * half, slope


def halves_of(own_ref, oth_ref, half, size):
    def pick(row):
        ref = own_ref if row < half else oth_ref
        return ref[row % half : row % half + size]

    return pick


def feed_kernel(
    x_own_ref, x_oth_ref, branch_ref, got_ref, gains_ref, biases_ref, cot_own_ref, cot_oth_ref,
    expand_hbm, shrink_hbm, far_hbm,
    middle_hbm, feed_hbm, feed_send_hbm, second_hbm, second_send_hbm, own_hbm, far_out_hbm,
    weights_ref, middle_ref, rows_ref, feed_ref, second_ref, feed_send_ref, second_send_ref,
    active_ref, hidden_ref, cot_ref, own_ref, far_ref, load_sem, store_sem,
):
    r = pl.program_id(0)
    length, width = rows_ref.shape
    half = length // 2
    units = active_ref.shape[1]
    loads = [
        pltpu.make_async_copy(source, weights_ref.at[i], load_sem.at[i])
        for i, source in enumerate((expand_hbm, shrink_hbm, far_hbm.at[0], far_hbm.at[1]))
    ]
    for load in loads:
        load.start()
    stores = []

    def store(source, target):
        copy = pltpu.make_async_copy(source, target.at[r], store_sem.at[len(stores)])
        copy.start()
        stores.append(copy)

    for row in range(0, length, HALF):
        here = slice(row, row + HALF)
        x_ref = x_own_ref if row < half else x_oth_ref
        there = (row + half) % length
        middle = (
            x_ref[row % half : row % half + HALF].astype(F32)
            + branch_ref[here]
            + got_ref[there : there + HALF].astype(F32)
        )
        middle_ref[here] = middle
        standard, _ = standardize(middle)
        rows_ref[here] = (standard * gains_ref[1:2] + biases_ref[1:2]).astype(BF)
    store(middle_ref, middle_hbm)
    cot_ref[:half] = cot_own_ref[...]
    cot_ref[half:] = cot_oth_ref[...]
    lower = ((0,), (0,))
    for quarter, grads_ref in enumerate((own_ref, far_ref)):
        expand_ref, shrink_ref = weights_ref.at[2 * quarter], weights_ref.at[2 * quarter + 1]
        loads[2 * quarter].wait()
        loads[2 * quarter + 1].wait()
        for row in range(0, length, TILE):
            here = slice(row, row + TILE)
            for unit in range(0, units, TILE):
                some = slice(unit, unit + TILE)
                active, slope = gelu_and_slope(dot(rows_ref[here], expand_ref[:, some]))
                active_ref[here, some] = active.astype(BF)
                hidden_ref[here, some] = (dot_t(cot_ref[here], shrink_ref[some]) * slope).astype(BF)
            feed = dot(active_ref[here], shrink_ref[...])
            second = dot_t(hidden_ref[here], expand_ref[...])
            if quarter == 1:
                feed = feed + feed_ref[here]
                second = second + second_ref[here]
                second_send_ref[here] = second.astype(BF)
                if row >= half:
                    feed_send_ref[row - half : row - half + TILE] = feed.astype(BF)
            feed_ref[here] = feed
            second_ref[here] = second
        if quarter == 1:
            store(second_ref, second_hbm)
            store(second_send_ref, second_send_hbm)
            store(feed_ref.at[:half], feed_hbm)
            store(feed_send_ref, feed_send_hbm)
        for unit in range(0, units, TILE):
            some = slice(unit, unit + TILE)
            grads_ref[0, some] = dot(hidden_ref[:, some], rows_ref[...], lower).astype(BF)
            grads_ref[1, some] = dot(active_ref[:, some], cot_ref[...], lower).astype(BF)
        store(grads_ref, own_hbm if quarter == 0 else far_out_hbm)
    for copy in stores:
        copy.wait()


def middle_kernel(
    t_ref, middle_ref, second_ref, got_ref, gains_ref, cot_own_ref, cot_oth_ref,
    own_ref, far_ref, att_own_ref, att_far_ref, *refs,
):
    grad_own_ref, to_own_ref, to_far_ref, out_own_ref, out_far_ref, sums_ref, branch_ref = refs
    length = middle_ref.shape[0]
    half = length // 2
    pick = halves_of(cot_own_ref, cot_oth_ref, half, WIDE)
    gain = bias = 0.0
    for row in range(0, length, WIDE):
        here = slice(row, row + WIDE)
        there = (row + half) % length
        grad = second_ref[here] + got_ref[there : there + WIDE].astype(F32)
        standard, scale = standardize(middle_ref[here])
        if row < half:
            gain = gain + jnp.sum(grad * standard, axis=0, keepdims=True)
            bias = bias + jnp.sum(grad, axis=0, keepdims=True)
        grad = pick(row).astype(F32) + norm_back(grad, standard, scale, gains_ref[1:2])
        if row < half:
            grad_own_ref[here] = grad
        branch = grad.astype(BF)
        branch_ref[here] = branch
        to_own_ref[here] = dot_t(branch, own_ref[...]).astype(BF)
        to_far_ref[here] = dot_t(branch, far_ref[...]).astype(BF)
    lower = ((0,), (0,))
    for ref in (to_own_ref, to_far_ref, grad_own_ref):
        complete(ref)
    out_own_ref[...] = dot(att_own_ref[...], branch_ref[...], lower).astype(BF)
    out_far_ref[...] = dot(att_far_ref[...], branch_ref[...], lower).astype(BF)
    sums_ref[0:1] = gain
    sums_ref[1:2] = bias


def first_back_kernel(
    rows_ref, grads_own_ref, grads_far_ref, grad_zero_ref, weight_own_ref, weight_far_ref,
    zero_ref, x_own_ref, x_oth_ref, out_own_ref, out_far_ref, feed_send_ref,
    handed_in_ref, first_ref, send_ref, own_ref, far_ref, sums_ref, handed_ref,
):
    length = rows_ref.shape[0]
    half = length // 2
    group = out_own_ref.shape[0]
    lower = ((0,), (0,))
    send_ref[0] = feed_send_ref[...]
    far_ref[:group] = dot(grads_far_ref[2], rows_ref[...], lower).astype(BF)
    far_ref[group:] = out_far_ref[...]
    own_ref[:group] = dot(grads_own_ref[2], rows_ref[...], lower).astype(BF)
    own_ref[group:] = out_own_ref[...]
    complete(far_ref)
    complete(own_ref)
    gain = bias = 0.0
    pick = halves_of(x_own_ref, x_oth_ref, half, TILE)
    for row in range(0, length, TILE):
        here = slice(row, row + TILE)
        first = 0.0
        for c in range(3):
            first = first + dot(grads_own_ref[c, here], weight_own_ref[c])
            first = first + dot(grads_far_ref[c, here], weight_far_ref[c])
        for c in range(2):
            first = first + dot(
                grad_zero_ref[c, here], zero_ref[c * HEAD_DIM : (c + 1) * HEAD_DIM]
            )
        standard, _ = standardize(pick(row).astype(F32))
        gain = gain + jnp.sum(first * standard, axis=0, keepdims=True)
        bias = bias + jnp.sum(first, axis=0, keepdims=True)
        if row < half:
            first_ref[here] = first
        else:
            send_ref[1, row - half : row - half + TILE] = first.astype(BF)
    sums_ref[0:1] = gain
    sums_ref[1:2] = bias


def early_kernel(
    t_ref, rows_ref, grads_own_ref, grads_far_ref, grad_zero_ref, zero_came_ref, small_ref, earlier_ref, *refs
):
    own_ref, far_ref, sum_ref = refs[1], refs[2], refs[-1]
    lower = ((0,), (0,))
    t = t_ref[0]
    length = rows_ref.shape[0]
    half = length // 2
    group = grads_own_ref.shape[2]
    for ref in (rows_ref, grad_zero_ref, zero_came_ref):
        ready(ref)
    for grads_ref, out_ref, place in ((grads_far_ref, far_ref, 2), (grads_own_ref, own_ref, 0)):
        for c in range(2):
            sum_ref[...] = grads_ref[c]

            @pl.when(t == place)
            def _():
                for start in (0, half):
                    here = slice(start, start + half)
                    there = slice(half - start, length - start)
                    share = grad_zero_ref[c, here].astype(F32) + zero_came_ref[c, there].astype(F32)
                    share = share + grads_ref[c, here, :HEAD_DIM].astype(F32)
                    sum_ref[here, :HEAD_DIM] = share.astype(BF)

            out_ref[c * group : (c + 1) * group] = dot(
                sum_ref[...], rows_ref[...], lower
            ).astype(BF)
        if place == 2:
            out_ref[2 * group :] = small_ref[...]
        complete(out_ref)


VMEM_LIMIT = 56 * 1024 * 1024
SMEM = pl.BlockSpec(memory_space=pltpu.SMEM)
ANY = pl.BlockSpec(memory_space=pl.ANY)
COST = pl.CostEstimate(flops=10**6, bytes_accessed=10**4, transcendentals=0)


def scratch(*shape, dtype=F32):
    return pltpu.VMEM(shape, dtype)


class Fetched:
    def __init__(self, source, ref, sem):
        self.copy, self.ref, self.waited = pltpu.make_async_copy(source, ref, sem), ref, False
        self.shape = ref.shape
        self.copy.start()

    def ready(self):
        if not self.waited:
            self.copy.wait()
            self.waited = True
        return self.ref

    def __getitem__(self, index):
        return self.ready()[index]

    @property
    def at(self):
        return self.ready().at


def complete(ref):
    if isinstance(ref, Written):
        ref.finish()


def ready(ref):
    if isinstance(ref, Fetched):
        ref.ready()


class Written:
    def __init__(self, target, ref, sem):
        self.copy, self.ref, self.sent = pltpu.make_async_copy(ref, target, sem), ref, False
        self.shape, self.dtype = ref.shape, ref.dtype

    def __getitem__(self, index):
        return self.ref[index]

    def __setitem__(self, index, value):
        self.ref[index] = value

    @property
    def at(self):
        return self.ref.at

    def finish(self):
        if not self.sent:
            self.copy.start()
            self.sent = True


def staged_kernel(kernel, kinds, staged_outs, extra, *refs):
    r = pl.program_id(0)
    count, handed = len(kinds), extra[0]
    ins, rest = refs[:count], refs[count:]
    handed_in, rest = rest[:handed], rest[handed:]
    outs, rest = rest[: extra[1]], rest[extra[1] :]
    handed_out, rest = rest[:handed], rest[handed:]
    plain, buffers = rest[: extra[2]], list(rest[extra[2] :])
    sem = buffers.pop()
    arguments, used = [], 0
    sources = {"row": lambda v: v.at[r], "whole": lambda v: v, "out": lambda v: v.at[3]}
    for kind, ref in zip(kinds, ins):
        if kind in sources:
            ref = Fetched(sources[kind](ref), buffers.pop(0), sem.at[used])
            used += 1
        arguments.append(ref)
    results = []
    for ref, big in zip(outs, staged_outs):
        if big:
            ref = Written(ref.at[r], buffers.pop(0), sem.at[used])
            used += 1
        results.append(ref)
    kernel(*arguments, *handed_in, *results, *handed_out, *plain)
    for ref in arguments:
        if isinstance(ref, Fetched):
            ref.ready()
    for ref in results:
        complete(ref)
    for ref in results:
        if isinstance(ref, Written):
            ref.copy.wait()


def whole(shape):
    return pl.BlockSpec(shape, lambda r: (0,) * len(shape))


def by_row(shape):
    return pl.BlockSpec((None,) + shape[1:], lambda r: (r,) + (0,) * (len(shape) - 1))


def third(shape):
    return pl.BlockSpec((None,) + shape[1:], lambda r: (3,) + (0,) * (len(shape) - 1))


def call(
    kernel, n, operands, outs, scratches, handed=(), placed=None, staged=True, cost=None
):
    arrays = [v for _, v in operands] + list(handed)
    kinds = [
        "block" if v.size < 2**16 or not staged else kind if kind != "block" else kind
        for kind, v in operands
    ]
    kinds = [old if old in ("smem", "any") else new for (old, _), new in zip(operands, kinds)]
    part = {"row": lambda s: s[1:], "whole": lambda s: s, "out": lambda s: s[1:]}
    buffers = [
        scratch(*part[k](v.shape), dtype=v.dtype) for k, (_, v) in zip(kinds, operands) if k in part
    ]
    big = [staged and placed is None and s[-2] >= 16 for s, _ in outs]
    buffers += [scratch(*s, dtype=d) for (s, d), b in zip(outs, big) if b]
    places = {"row": by_row, "whole": whole, "out": third}
    specs = [
        SMEM if old == "smem" else places[old](v.shape) if k == "block" else ANY
        for k, (old, v) in zip(kinds, operands)
    ]
    return pl.pallas_call(
        partial(staged_kernel, kernel, kinds, big, (len(handed), len(outs), len(scratches))),
        grid=(n,),
        in_specs=specs + [ANY] * len(handed),
        out_specs=[
            ANY if b or placed is not None else by_row((n,) + s) for (s, _), b in zip(outs, big)
        ]
        + [ANY] * len(handed),
        out_shape=[jax.ShapeDtypeStruct((n,) + s, d) for s, d in outs]
        + [jax.ShapeDtypeStruct(v.shape, v.dtype) for v in handed],
        scratch_shapes=scratches + buffers + [pltpu.SemaphoreType.DMA((max(len(buffers), 1),))],
        input_output_aliases={len(operands) + i: len(outs) + i for i in range(len(handed))},
        compiler_params=pltpu.CompilerParams(vmem_limit_bytes=VMEM_LIMIT),
        cost_estimate=cost or COST,
    )(*arrays)


def idle_kernel(*refs):
    del refs


def after(value, *earlier):
    return pl.pallas_call(
        idle_kernel,
        in_specs=[ANY] * (1 + len(earlier)),
        out_specs=ANY,
        out_shape=jax.ShapeDtypeStruct(value.shape, value.dtype),
        input_output_aliases={0: 0},
        cost_estimate=COST,
    )(value, *earlier)


def attend_first(t, x_own, x_oth, gains, biases, weight, segments):
    n, _, width = x_own.shape
    length, group, span = segments.shape[1], weight.shape[1], (REACH + 1) * TILE
    return call(
        first_kernel,
        n,
        [
            ("smem", t),
            ("row", x_own),
            ("row", x_oth),
            ("whole", gains),
            ("whole", biases),
            ("whole", weight),
            ("row", segments.astype(F32)[:, None, :]),
        ],
        [
            ((length, width), BF),
            ((3, length, group), BF),
            ((2, length, HEAD_DIM), BF),
            ((length, span), F32),
            ((length, group), BF),
            ((length, 128), F32),
            ((1, 128), F32),
            ((2 * HEAD_DIM, width), BF),
        ],
        [
            scratch(3, TILE, span),
            scratch(3, TILE, span, dtype=BF),
            scratch(TILE, span, dtype=BF),
            scratch(TILE, span, dtype=BF),
            scratch(1, length),
            scratch(length, 8),
        ],
        staged=False,
    )


def attend_second(t, rows, weight_own, weight_far, pm, att_own):
    n, length, width = rows.shape
    group, span = weight_far.shape[1], pm.shape[2]
    return call(
        second_kernel,
        n,
        [
            ("smem", t),
            ("row", rows),
            ("whole", weight_own),
            ("whole", weight_far),
            ("row", pm),
            ("row", att_own),
        ],
        [
            ((3, length, group), BF),
            ((length, group), BF),
            ((length, 128), F32),
            ((length, width), F32),
            ((length, width), BF),
        ],
        [scratch(3, TILE, span), scratch(3, TILE, span, dtype=BF)],
        staged=False,
    )


def attend_back(t, qkv, zqk, pm, lse, grad, before=None):
    n, _, length, group = qkv.shape
    span = pm.shape[2]
    operands = [("smem", t)] + [("row", v) for v in (qkv, zqk, pm, lse, grad)]
    if before is not None:
        operands.append(("row", before))
    return call(
        partial(backward_kernel, before is not None),
        n,
        operands,
        [
            ((3, length, group), BF),
            ((2, length, HEAD_DIM), F32 if before is None else BF),
        ],
        [
            scratch(3, TILE, span),
            scratch(3, TILE, span),
            scratch(3, TILE, span, dtype=BF),
            scratch(3, TILE, span, dtype=BF),
            scratch(TILE, span),
            scratch(TILE, span, dtype=BF),
            scratch(TILE, span, dtype=BF),
            scratch(TILE, span, dtype=BF),
            scratch(group, length),
            scratch(group, length),
            scratch(HEAD_DIM, length),
            scratch(length, HEAD_DIM),
            scratch(1, length),
        ],
        staged=False,
    )


def feed_forward(x_own, x_oth, branch, got, gains, biases, cot_own, cot_oth, expand, shrink, far):
    n, length, width = branch.shape
    units = expand.shape[1]
    half = length // 2
    return call(
        feed_kernel,
        n,
        [("row", v) for v in (x_own, x_oth, branch, got)]
        + [("whole", gains), ("whole", biases), ("row", cot_own), ("row", cot_oth)]
        + [("any", expand), ("any", shrink), ("any", far)],
        [
            ((length, width), F32),
            ((half, width), F32),
            ((half, width), BF),
            ((length, width), F32),
            ((length, width), BF),
            ((2, units, width), BF),
            ((2, units, width), BF),
        ],
        [
            scratch(4, units, width, dtype=BF),
            scratch(length, width),
            scratch(length, width, dtype=BF),
            scratch(length, width),
            scratch(length, width),
            scratch(half, width, dtype=BF),
            scratch(length, width, dtype=BF),
            scratch(length, units, dtype=BF),
            scratch(length, units, dtype=BF),
            scratch(length, width, dtype=BF),
            scratch(2, units, width, dtype=BF),
            scratch(2, units, width, dtype=BF),
            pltpu.SemaphoreType.DMA((4,)),
            pltpu.SemaphoreType.DMA((7,)),
        ],
        placed=ANY,
        staged=False,
    )


def middle_back(t, middle, second, got, gains, cot_own, cot_oth, weight_own, weight_far, att_own, att_far):
    n, length, width = middle.shape
    group = weight_far.shape[1]
    return call(
        middle_kernel,
        n,
        [
            ("smem", t),
            ("row", middle),
            ("row", second),
            ("row", got),
            ("whole", gains),
            ("row", cot_own),
            ("row", cot_oth),
            ("whole", weight_own),
            ("out", weight_far),
            ("row", att_own),
            ("row", att_far),
        ],
        [
            ((length // 2, width), F32),
            ((length, group), BF),
            ((length, group), BF),
            ((group, width), BF),
            ((group, width), BF),
            ((2, width), F32),
        ],
        [scratch(length, width, dtype=BF)],
        staged=False,
    )


def first_back(
    rows, grads_own, grads_far, grad_zero, weight_own, weight_far, zero,
    x_own, x_oth, out_own, out_far, feed_send, handed,
):
    n, length, width = rows.shape
    group = weight_far.shape[1]
    return call(
        first_back_kernel,
        n,
        [
            ("row", rows),
            ("row", grads_own),
            ("row", grads_far),
            ("row", grad_zero),
            ("whole", weight_own),
            ("whole", weight_far),
            ("whole", zero),
            ("row", x_own),
            ("row", x_oth),
            ("row", out_own),
            ("row", out_far),
            ("row", feed_send),
        ],
        [
            ((length // 2, width), F32),
            ((2, length // 2, width), BF),
            ((2 * group, width), BF),
            ((2 * group, width), BF),
            ((2, width), F32),
        ],
        [],
        (handed,),
        staged=False,
    )


def early_products(t, rows, grads_own, grads_far, grad_zero, zero_came, small, earlier, handed):
    n, length, width = rows.shape
    group = grads_own.shape[3]
    return call(
        early_kernel,
        n,
        [
            ("smem", t),
            ("row", rows),
            ("row", grads_own),
            ("row", grads_far),
            ("row", grad_zero),
            ("row", zero_came),
            ("row", small),
            ("any", earlier),
        ],
        [((2 * group, width), BF), ((2 * group + small.shape[1], width), BF)],
        [scratch(length, group, dtype=BF)],
        handed,
        staged=False,
        cost=pl.CostEstimate(
            flops=4 * 10**9, bytes_accessed=24 * 10**6, transcendentals=0
        ),
    )


def per_device(
    layer_input,
    cotangent,
    segment_ids,
    norm_gains,
    norm_biases,
    attend_weight,
    output_weight,
    expand_weight,
    shrink_weight,
):
    t = lax.axis_index("tensor")
    chip = t // 2
    core = t % 2
    rows, block, width = layer_input.shape
    n = rows // 2
    length = segment_ids.shape[1]
    half = length // 2
    units = expand_weight.shape[1]
    size, dp = lax.axis_size("tensor"), lax.axis_size("dp")
    across = [(i, i ^ 2) for i in range(size)]
    beside = [(i, i ^ 1) for i in range(size)]
    pairs = [[i, i ^ 2] for i in range(size) if i < i ^ 2]

    def swap_chip(v):
        return lax.ppermute(v, "tensor", across)

    def swap_core(v):
        return lax.ppermute(v, "tensor", beside)

    def mine(v):
        return lax.dynamic_slice_in_dim(v, chip * n, n, 0)

    def theirs(v):
        return lax.dynamic_slice_in_dim(v, (1 - chip) * n, n, 0)

    zero_own = attend_weight[:2, :, :HEAD_DIM].transpose(0, 2, 1).reshape(2 * HEAD_DIM, width)
    zero_low = jnp.where(chip == 0, zero_own, lax.ppermute(zero_own, "tensor", [(0, 2)]))
    zero_low = jnp.broadcast_to(zero_low, (n, *zero_low.shape))
    x_own = jnp.concatenate(
        [mine(layer_input), swap_chip(theirs(layer_input)), zero_low], axis=1
    )
    x_oth = swap_core(x_own)
    index = lax.axis_index("dp")
    cut = units // dp
    pieces = jnp.stack(
        [lax.dynamic_slice_in_dim(v, index * cut, cut, 0) for v in (expand_weight, shrink_weight)]
    )
    far_feed = lax.all_gather(after(swap_chip(pieces), x_own), "dp", axis=1, tiled=True)
    group = output_weight.shape[0]
    attend_own = attend_weight.transpose(0, 2, 1)
    weight_far = swap_chip(
        jnp.concatenate([attend_own, output_weight.reshape(1, group, width)])
    )
    segments = mine(segment_ids)

    t_array = t.reshape(1)
    first_rows, qkv_own, zqk, pm, att_own, lse_own, kept, zero_weight = attend_first(
        t_array, x_own, x_oth, norm_gains, norm_biases, attend_own, segments
    )
    zero_weight = zero_weight[0]
    cot_came = swap_chip(after(theirs(cotangent), first_rows))
    cot_own = jnp.concatenate([mine(cotangent), cot_came], axis=1)
    cot_oth = swap_core(cot_own)
    qkv_far, att_far, lse_far, branch, branch_send = attend_second(
        t_array, first_rows, output_weight, weight_far, pm, att_own
    )
    middle, feed, feed_send, second, second_send, feed_grads_own, feed_grads_far = feed_forward(
        x_own, x_oth, branch, swap_core(after(branch_send, cot_own)), norm_gains, norm_biases,
        cot_own, cot_oth, expand_weight, shrink_weight, far_feed,
    )

    def over_rows(v):
        return v[0] if n == 1 else jnp.sum(v.astype(F32), axis=0).astype(BF)

    second_came = swap_core(second_send)
    feed_grads_came = swap_chip(over_rows(feed_grads_far))
    grad_middle, to_own, to_far, out_own, out_far, sums_second = middle_back(
        t_array, middle, second, second_came, norm_gains, cot_own, cot_oth,
        output_weight, weight_far, att_own, att_far,
    )

    def total(a, b):
        return (a.astype(F32) + b.astype(F32)).astype(BF)

    def packed(small):
        high = small.astype(BF)
        low = (small - high.astype(F32)).astype(BF)
        both = jnp.concatenate([high, low])
        return jnp.pad(both, ((0, 16 - both.shape[0]), (0, 0)))

    def unpacked(both):
        return both[:5].astype(F32) + both[5:10].astype(F32)

    def over_dp(v, small=None, order=(), wait=None, noted=None, sends=None):
        steps = [1 << k for k in range(dp.bit_length() - 1)]
        steps = [k for k in order if k in steps] + [k for k in steps if k not in order]
        for step in steps:
            upper = (index // step) % 2
            part = v.shape[0] // 2
            keep = lax.dynamic_slice_in_dim(v, upper * part, part, 0)
            send = lax.dynamic_slice_in_dim(v, (1 - upper) * part, part, 0)
            if small is not None:
                send = jnp.concatenate([send, packed(small)])
            if sends is not None:
                sends.append(send)
            came = lax.ppermute(send, "dp", [(i, i ^ step) for i in range(dp)])
            v = total(keep, came[:part])
            if sends is not None:
                sums.append(v)
            if small is not None:
                small = small + unpacked(came[part:])
        for step in reversed(steps):
            upper = (index // step) % 2
            if wait is not None and step == steps[0]:
                v = after(v, wait)
            if noted is not None:
                noted.append(v)
            came = lax.ppermute(v, "dp", [(i, i ^ step) for i in range(dp)])
            if noted is not None and step == steps[0]:
                v = jnp.where(upper == 0, v, came), jnp.where(upper == 0, came, v)
            else:
                v = jnp.where(upper == 0, jnp.concatenate([v, came]), jnp.concatenate([came, v]))
        return v, small

    grads_far, zero_far = attend_back(t_array, qkv_far, zqk, pm, lse_far, to_far)
    grads_own, grad_zero = attend_back(t_array, qkv_own, zqk, pm, lse_own, to_own, zero_far)
    zero_came = lax.ppermute(grad_zero, "tensor", [(1, 0), (3, 2)])
    first, first_send, own_late, far_late, sums_first, feed_grads_own = first_back(
        first_rows, grads_own, grads_far, grad_zero, attend_own, weight_far, zero_weight,
        x_own, x_oth, out_own, out_far, feed_send, feed_grads_own,
    )
    feed_grads_own = over_rows(feed_grads_own)
    feed_sums = [total(feed_grads_own[i], feed_grads_came[i]) for i in range(2)]
    sends, sums = [], []
    grad_expand, _ = over_dp(feed_sums[0], None, (), None, None, sends)
    far_late = over_rows(far_late)
    late_came = swap_chip(far_late)
    sums_first, sums_second = jnp.sum(sums_first, axis=0), jnp.sum(sums_second, axis=0)
    small = jnp.stack(
        [
            sums_first[0],
            sums_second[0],
            sums_first[1],
            sums_second[1],
            jnp.full((width,), 0.5 * jnp.sum(kept[:, 0, 0]), F32),
        ]
    )
    small_rows = jnp.broadcast_to(packed(small), (n, 16, width))
    own_early, far_early, own_late = early_products(
        t_array, after(first_rows, far_late), grads_own, grads_far, grad_zero, zero_came, small_rows,
        sends[0], (own_late,),
    )
    came = swap_core(first_send)
    came = after(came, sums[min(1, len(sums) - 1)]).astype(F32)
    far_early = (
        far_early[0]
        if n == 1
        else jnp.concatenate([over_rows(far_early[:, : 2 * group]), packed(small)])
    )
    early_came = swap_chip(far_early)
    small = small + unpacked(early_came[2 * group :])
    proj = jnp.concatenate(
        [
            total(over_rows(own_early), early_came[: 2 * group]),
            total(over_rows(own_late), late_came),
        ]
    )
    noted = []
    (grad_early, grad_late), small = over_dp(proj, small, (), None, noted)
    small = small + swap_core(small)
    grad_shrink, _ = over_dp(feed_sums[1], None, (2, 1), noted[max(len(noted) - 2, 0)])

    layer_own = (middle[:, :half] + feed + came[:, 0]).astype(BF)
    standard_first, scale_first = standardize(x_own[:, :half].astype(F32))
    input_part = norm_back(first + came[:, 1], standard_first, scale_first, norm_gains[0])
    input_own = (grad_middle + input_part).astype(BF)
    results = jnp.stack([layer_own, input_own])
    home = swap_chip(results[:, :, block:])
    stays = results[:, :, :block]
    low, high = jnp.where(chip == 0, stays, home), jnp.where(chip == 0, home, stays)
    results = jnp.concatenate([low, high], axis=1)
    grad_attend = jnp.concatenate([grad_early, grad_late[:group]]).astype(F32)
    grad_attend = grad_attend.reshape(3, group, width).transpose(0, 2, 1)
    grad_output = grad_late[group:].astype(F32)
    kept_fraction = small[4, 0] / (rows * length * dp)
    return (
        results[0],
        results[1],
        small[:2],
        small[2:4],
        grad_attend,
        grad_output,
        grad_expand.astype(F32).T,
        grad_shrink.astype(F32),
        kept_fraction,
    )


def solution(mesh):
    return jax.shard_map(
        per_device,
        mesh=mesh,
        in_specs=(
            P("dp", "tensor", None),
            P("dp", "tensor", None),
            P("dp", None),
            P(),
            P(),
            P(None, None, "tensor"),
            P("tensor", None),
            P(None, "tensor"),
            P("tensor", None),
        ),
        out_specs=(
            P("dp", "tensor", None),
            P("dp", "tensor", None),
            P(),
            P(),
            P(None, None, "tensor"),
            P("tensor", None),
            P(None, "tensor"),
            P("tensor", None),
            P(),
        ),
        check_vma=False,
    )
```
